32 devices in a mesh: pts: 2 (over x), col: 16 (over z, y, core).
Axes of the slice: x: 2, y: 2, z: 4, core: 2. Of those that a mesh axis runs over, the one named last changes fastest.
Arguments:
- rhs_child: float32 [5248, 2, 128], P('col'), may hold values from -6 to 6
- rhs_root: float32 [10496, 2, 128], P('col'), may hold values from -6 to 6
- lower_kids: bfloat16 [4, 5248, 5248], P('pts', None, 'col'), parts along dimension 0, may hold values from -0.0625 to 0.0625
- lower_couple: bfloat16 [4, 5248, 10496], P('pts', None, 'col'), parts along dimension 0, may hold values from -0.078125 to 0.078125
- lower_root: bfloat16 [4, 10496, 10496], P('pts', 'col'), parts along dimension 0, may hold values from -0.0390625 to 0.0390625
- upper_root: bfloat16 [4, 10496, 10496], P('pts', 'col'), parts along dimension 0, may hold values from -0.0390625 to 0.0390625
- upper_couple: bfloat16 [4, 10496, 5248], P('pts', 'col'), parts along dimension 0, may hold values from -0.0625 to 0.0625
- upper_kids: bfloat16 [4, 5248, 5248], P('pts', None, 'col'), parts along dimension 0, may hold values from -0.0625 to 0.0625
- tile_pattern: int32 [656, 328], replicated, may hold values 0 or 1
Outputs:
- child_solution: float32 [10496, 2, 128], P(('pts', 'col')), parts along dimension 0
- root_solution: float32 [20992, 2, 128], P(('pts', 'col')), parts along dimension 0
The draws below stay inside these ranges and needn't reach their ends.
There are 2 independent parts, one for each index of `pts`. The reference program is written for one: setup_inputs(seed, part) draws one part's arguments, and reference() takes and returns one part's arrays. A program takes and returns all parts, laid end to end along the dimension named above; an argument that names none is the same for every part. Nothing has to cross between parts.
All inputs are finite; a program needn't handle non-finite values.
Results may differ from the reference program's by a relative error of at most 0.0065.
Values may be sent and summed in bfloat16 or wider, within the bound.
No kernel may reach another device: no remote copies, remote signals or barrier semaphores. Data moves between devices by JAX's collectives and lax.ppermute only.
A program may use at most 192 MiB of HBM per device.

```python
import jax
import jax.numpy as jnp
from jax import lax

P_SIZE = 128
N1 = 5248
N0 = 10496
NB = 16


def with_ends(drawn, own_key, least, largest):
    place = [jax.random.randint(jax.random.fold_in(own_key, axis), (), 0, length) for axis, length in enumerate(drawn.shape)]
    longest = drawn.shape.index(max(drawn.shape))
    neighbour = place[:longest] + [(place[longest] + 1) % drawn.shape[longest]] + place[longest + 1:]
    return drawn.at[tuple(place)].set(least).at[tuple(neighbour)].set(largest)


def levels(key, extent, cuts, least, top_value):
    def one(axis_at, shards_of):
        draws = jax.random.uniform(jax.random.fold_in(jax.random.fold_in(key, 6), axis_at), (shards_of,), jnp.float32, least / len(cuts), top_value / len(cuts))
        return jnp.repeat(jnp.exp(draws), extent[axis_at] // shards_of).reshape((-1,) + (1,) * (len(extent) - axis_at - 1))

    factor_of = one(*cuts[0])
    for cut in cuts[1:]:
        factor_of = factor_of * one(*cut)
    return factor_of


def normal_values(key, extent, deviation, bound, pieces=(), held_as=jnp.bfloat16):
    level = levels(key, extent, pieces, -0.22, 0.18) if pieces else 1.0
    entries = jax.random.normal(key, extent, jnp.float32) * deviation * level
    return jnp.minimum(jnp.maximum(entries, -bound), bound).astype(held_as)


def setup_inputs(seed: int = 0, part: int = 0) -> dict:
    streams_of = jax.random.split(jax.random.key(seed), 10)
    part_keys = jax.random.split(jax.random.fold_in(streams_of[9], part), 10)
    return {
        "rhs_child": normal_values(streams_of[0], (N1, 2, P_SIZE), 1.0, 6.0, ((0, 16),), jnp.float32),
        "rhs_root": normal_values(streams_of[1], (N0, 2, P_SIZE), 1.0, 6.0, ((0, 16),), jnp.float32),
        "lower_kids": normal_values(part_keys[2], (2, N1, N1), (2 * N1) ** -0.5, 0.0625, ((2, 16),)),
        "lower_couple": normal_values(part_keys[3], (2, N1, N0), N1 ** -0.5, 0.078125, ((2, 16),)),
        "lower_root": normal_values(part_keys[4], (2, N0, N0), (2 * N0) ** -0.5, 0.0390625, ((1, 16),)),
        "upper_root": normal_values(part_keys[5], (2, N0, N0), (2 * N0) ** -0.5, 0.0390625, ((1, 16),)),
        "upper_couple": normal_values(part_keys[6], (2, N0, N1), N0 ** -0.5, 0.0625, ((1, 16),)),
        "upper_kids": normal_values(part_keys[7], (2, N1, N1), (2 * N1) ** -0.5, 0.0625, ((2, 16),)),
        "tile_pattern": with_ends((jax.random.randint(streams_of[8], (N0 // NB, N1 // NB), 0, 2) < 1).astype(jnp.int32), jax.random.fold_in(streams_of[8], 1), 0, 1),
    }


def combine(product):
    return jnp.stack([product[..., 0, 0, :] - product[..., 1, 1, :], product[..., 0, 1, :] + product[..., 1, 0, :]], axis=-2)


def reference(rhs_child, rhs_root, lower_kids, lower_couple, lower_root, upper_root, upper_couple, upper_kids, tile_pattern):
    high = lax.Precision.HIGHEST
    maskf = jnp.repeat(jnp.repeat(tile_pattern.astype(jnp.float32), NB, axis=0), NB, axis=1)
    lower_masked = lower_couple.astype(jnp.float32) * jnp.transpose(maskf)[None]
    upper_masked = upper_couple.astype(jnp.float32) * maskf[None]
    child_in = rhs_child.astype(jnp.bfloat16).astype(jnp.float32)
    child_lower = combine(jnp.einsum("aji,jbp->iabp", lower_kids.astype(jnp.float32), child_in, precision=high))
    child_lower_b = child_lower.astype(jnp.bfloat16).astype(jnp.float32)
    root_rhs = rhs_root - combine(jnp.einsum("aji,jbp->iabp", lower_masked, child_lower_b, precision=high))
    root_rhs_b = root_rhs.astype(jnp.bfloat16).astype(jnp.float32)
    root_lower = combine(jnp.einsum("aic,cbp->iabp", lower_root.astype(jnp.float32), root_rhs_b, precision=high))
    root_lower_b = root_lower.astype(jnp.bfloat16).astype(jnp.float32)
    root_solution = combine(jnp.einsum("aic,cbp->iabp", upper_root.astype(jnp.float32), root_lower_b, precision=high))
    root_solution_b = root_solution.astype(jnp.bfloat16).astype(jnp.float32)
    child_rhs = child_lower - combine(jnp.einsum("aij,ibp->jabp", upper_masked, root_solution_b, precision=high))
    child_rhs_b = child_rhs.astype(jnp.bfloat16).astype(jnp.float32)
    child_solution = combine(jnp.einsum("aji,jbp->iabp", upper_kids.astype(jnp.float32), child_rhs_b, precision=high))
    return child_solution, root_solution
```

```python
import functools

import jax
import jax.numpy as jnp
import numpy as np
from jax import lax
from jax.experimental import pallas as pl
from jax.experimental.pallas import tpu as pltpu
from jax.sharding import PartitionSpec as P

NB = 16
GROUP = 16
LANES = 128
TILE_ROWS = 64
FIRST, NEXT = 10, 18
AHEAD = 2
VMEM = 62 * 1024 * 1024


def combine(product):
    return jnp.stack(
        [
            product[..., 0, 0, :] - product[..., 1, 1, :],
            product[..., 0, 1, :] + product[..., 1, 0, :],
        ],
        axis=-2,
    )


def column_fold(matrix, piece):
    return combine(jnp.einsum("aji,jbp->iabp", matrix, piece, preferred_element_type=jnp.float32))


def root_fold(matrix, piece):
    return combine(jnp.einsum("aic,cbp->iabp", matrix, piece, preferred_element_type=jnp.float32))


def general_shards(
    rhs_child,
    rhs_root,
    lower_kids,
    lower_couple,
    lower_root,
    upper_root,
    upper_couple,
    upper_kids,
    tile_pattern,
):
    root_rows = rhs_root.shape[0]
    position = lax.axis_index("col")
    pattern_f = tile_pattern.astype(jnp.float32)
    root_tiles = (position * root_rows + jnp.arange(root_rows, dtype=jnp.int32)) // NB
    root_onehot = (
        root_tiles[:, None] == jnp.arange(pattern_f.shape[0], dtype=jnp.int32)[None, :]
    ).astype(jnp.float32)
    couple_mask = jnp.repeat(jnp.dot(root_onehot, pattern_f), NB, axis=1)
    child_in = rhs_child.astype(jnp.bfloat16)
    child_lower = column_fold(lower_kids, lax.all_gather(child_in, "col", axis=0, tiled=True))
    child_lower_b = child_lower.astype(jnp.bfloat16)
    masked = lower_couple * jnp.transpose(couple_mask).astype(jnp.bfloat16)[None]
    coupling = column_fold(masked, lax.all_gather(child_lower_b, "col", axis=0, tiled=True))
    root_rhs_b = (rhs_root - coupling).astype(jnp.bfloat16)
    root_lower = root_fold(lower_root, lax.all_gather(root_rhs_b, "col", axis=0, tiled=True))
    root_lower_b = root_lower.astype(jnp.bfloat16)
    root_solution = root_fold(upper_root, lax.all_gather(root_lower_b, "col", axis=0, tiled=True))
    root_solution_b = root_solution.astype(jnp.bfloat16)
    masked = upper_couple * couple_mask.astype(jnp.bfloat16)[None]
    update = lax.psum_scatter(
        combine(
            jnp.einsum("aij,ibp->jabp", masked, root_solution_b, preferred_element_type=jnp.float32)
        ),
        "col",
        scatter_dimension=0,
        tiled=True,
    )
    child_rhs_b = (child_lower - update).astype(jnp.bfloat16)
    child_solution = column_fold(upper_kids, lax.all_gather(child_rhs_b, "col", axis=0, tiled=True))
    return (child_solution, root_solution)


def swap(x, bits):
    return lax.ppermute(x, "col", [(i, i ^ bits) for i in range(GROUP)])


def gather_pieces(x):
    pieces = {0: x}
    for bits in (12, 8, 4):
        pieces[bits] = swap(x, bits)
    pieces[2] = swap(x, 2)
    for bits in (4, 8, 12):
        pieces[bits | 2] = swap(pieces[bits], 2)
    for bits in (0, 2, 4, 8, 6, 10, 12, 14):
        pieces[bits | 1] = swap(pieces[bits], 1)
    return [pieces[m] for m in range(GROUP)]


def steps_of(depth):
    units = depth // LANES
    sizes = [min(FIRST, units)]
    units -= sizes[0]
    parts = -(-units // NEXT)
    sizes += [units // parts + (i < units % parts) for i in range(parts)]
    starts = np.cumsum([0, *sizes])
    return [(int(start) * LANES, size * LANES) for start, size in zip(starts, sizes)]


def fold_kernel(masked, residual, wide, narrow, *refs):
    refs = list(refs)
    place_ref = refs.pop(0)
    pieces = [refs.pop(0) for _ in range(GROUP)]
    w_hbm = refs.pop(0)
    if masked:
        rows_ref, tiles_ref = refs.pop(0), refs.pop(0)
    if residual:
        base_ref = refs.pop(0)
    wide_ref = refs.pop(0) if wide else None
    narrow_ref = refs.pop(0) if narrow else None
    x_ref, w_ref, acc_ref, piece_sems, w_sems = refs[:5]
    stage_ref = refs[5] if len(refs) > 5 else None

    place = place_ref[0]
    rows = pieces[0].shape[0]
    depth = w_hbm.shape[2]
    steps = steps_of(depth)

    def piece_copy(m):
        if stage_ref is None:
            start = pl.multiple_of((place ^ m) * rows, 16)
            target = x_ref.at[pl.ds(start, rows), :]
        else:
            target = stage_ref.at[m]
        return pltpu.make_async_copy(pieces[m], target, piece_sems.at[m])

    def w_copy(step):
        span = pl.ds(*steps[step])
        return pltpu.make_async_copy(w_hbm.at[:, :, span], w_ref.at[:, :, span], w_sems.at[step])

    for m in range(GROUP):
        piece_copy(m).start()
    for step in range(min(AHEAD, len(steps))):
        w_copy(step).start()
    acc_ref[...] = jnp.zeros_like(acc_ref)
    for m in range(GROUP):
        piece_copy(m).wait()
    if stage_ref is not None:
        low = (place & 1) == 0
        for m in range(0, GROUP, 2):
            mine = stage_ref[m].astype(jnp.float32)
            other = stage_ref[m + 1].astype(jnp.float32)
            pair = jnp.concatenate([jnp.where(low, mine, other), jnp.where(low, other, mine)], axis=0)
            start = pl.multiple_of(((place ^ m) >> 1) * (2 * rows), 16)
            x_ref[pl.ds(start, 2 * rows), :] = pair.astype(jnp.bfloat16)

    def multiply(start, size):
        span = pl.ds(start, size)
        x = x_ref[span, :]
        if masked:
            mask = jnp.dot(
                rows_ref[...], tiles_ref[:, span], preferred_element_type=jnp.float32
            ).astype(jnp.bfloat16)
        for part in range(2):
            w = w_ref[part, :, span]
            if masked:
                w = w * mask
            acc_ref[part] += jnp.dot(w, x, preferred_element_type=jnp.float32)

    for step in range(len(steps)):
        w_copy(step).wait()
        if step + AHEAD < len(steps):
            w_copy(step + AHEAD).start()
        multiply(*steps[step])
    half = acc_ref.shape[2] // 2
    real = acc_ref[0, :, :half] - acc_ref[1, :, half:]
    imag = acc_ref[0, :, half:] + acc_ref[1, :, :half]
    if residual:
        real = base_ref[:, :half] - real
        imag = base_ref[:, half:] - imag
    for out in (wide_ref, narrow_ref):
        if out is not None:
            out[:, :half] = real.astype(out.dtype)
            out[:, half:] = imag.astype(out.dtype)


def fold(place, pieces, matrix, mask=None, base=None, wide=False, narrow=True):
    _, height, depth = matrix.shape
    width = pieces[0].shape[1]
    rows = pieces[0].shape[0]
    anywhere = pl.BlockSpec(memory_space=pl.ANY)
    vmem = pl.BlockSpec(memory_space=pltpu.VMEM)
    operands = [place, *pieces, matrix]
    specs = [pl.BlockSpec(memory_space=pltpu.SMEM)] + [anywhere] * (GROUP + 1)
    if mask is not None:
        operands += list(mask)
        specs += [vmem, vmem]
    if base is not None:
        operands.append(base)
        specs.append(vmem)
    shapes = []
    if wide:
        shapes.append(jax.ShapeDtypeStruct((height, width), jnp.float32))
    if narrow:
        shapes.append(jax.ShapeDtypeStruct((height, width), jnp.bfloat16))
    scratch = [
        pltpu.VMEM((depth, width), jnp.bfloat16),
        pltpu.VMEM(matrix.shape, jnp.bfloat16),
        pltpu.VMEM((2, height, width), jnp.float32),
        pltpu.SemaphoreType.DMA((GROUP,)),
        pltpu.SemaphoreType.DMA((len(steps_of(depth)),)),
    ]
    if rows % 16:
        scratch.append(pltpu.VMEM((GROUP, rows, width), jnp.bfloat16))
    return pl.pallas_call(
        functools.partial(fold_kernel, mask is not None, base is not None, wide, narrow),
        out_shape=shapes,
        in_specs=specs,
        out_specs=[vmem] * len(shapes),
        scratch_shapes=scratch,
        compiler_params=pltpu.CompilerParams(vmem_limit_bytes=VMEM),
        cost_estimate=pl.CostEstimate(
            flops=4 * height * depth * width,
            bytes_accessed=2 * matrix.size + 2 * depth * width,
            transcendentals=0,
        ),
    )(*operands)


def spread_kernel(place_ref, x_ref, w_hbm, rows_ref, tiles_ref, keep_ref, send_ref, w_ref, total_ref, w_sems):
    place = place_ref[0]
    chips, rows, width = keep_ref.shape
    half = width // 2
    steps = steps_of(w_hbm.shape[2])

    def w_copy(step):
        span = pl.ds(*steps[step])
        return pltpu.make_async_copy(w_hbm.at[:, :, span], w_ref.at[:, :, span], w_sems.at[step])

    for step in range(min(AHEAD, len(steps))):
        w_copy(step).start()
    x = x_ref[...]
    for step in range(len(steps)):
        w_copy(step).wait()
        if step + AHEAD < len(steps):
            w_copy(step + AHEAD).start()
        span = pl.ds(*steps[step])
        mask = jnp.dot(
            rows_ref[...], tiles_ref[:, span], preferred_element_type=jnp.float32
        ).astype(jnp.bfloat16)
        first, second = (
            lax.dot_general(
                w_ref[part, :, span] * mask,
                x,
                (((0,), (0,)), ((), ())),
                preferred_element_type=jnp.float32,
            )
            for part in range(2)
        )
        total_ref[span, :half] = first[:, :half] - second[:, half:]
        total_ref[span, half:] = first[:, half:] + second[:, :half]
    low = (place & 1) == 0
    for q in range(chips):
        start = pl.multiple_of(((place >> 1) ^ q) * (2 * rows), 8)
        one = total_ref[pl.ds(start, rows), :]
        two = total_ref[pl.ds(start + rows, rows), :]
        keep_ref[q] = jnp.where(low, one, two)
        send_ref[q] = jnp.where(low, two, one).astype(send_ref.dtype)


def spread(place, x, matrix, mask):
    _, depth, length = matrix.shape
    chips = GROUP // 2
    width = x.shape[1]
    vmem = pl.BlockSpec(memory_space=pltpu.VMEM)
    block = (chips, length // GROUP, width)
    return pl.pallas_call(
        spread_kernel,
        out_shape=[
            jax.ShapeDtypeStruct(block, jnp.float32),
            jax.ShapeDtypeStruct(block, jnp.bfloat16),
        ],
        in_specs=[
            pl.BlockSpec(memory_space=pltpu.SMEM),
            vmem,
            pl.BlockSpec(memory_space=pl.ANY),
            vmem,
            vmem,
        ],
        out_specs=[vmem, vmem],
        scratch_shapes=[
            pltpu.VMEM(matrix.shape, jnp.bfloat16),
            pltpu.VMEM((length, width), jnp.float32),
            pltpu.SemaphoreType.DMA((len(steps_of(length)),)),
        ],
        compiler_params=pltpu.CompilerParams(vmem_limit_bytes=VMEM),
        cost_estimate=pl.CostEstimate(
            flops=4 * length * depth * width,
            bytes_accessed=2 * matrix.size + 3 * length * width,
            transcendentals=0,
        ),
    )(place, x, matrix, *mask)


def scatter_sum(keep, send):
    across = {}
    for z in (3, 2, 1, 0):
        got = swap(send[2 * z : 2 * z + 2], 1).astype(jnp.float32)
        mine = keep[2 * z] + got[0]
        other = keep[2 * z + 1] + got[1]
        across[z] = mine + swap(other.astype(jnp.bfloat16), 2).astype(jnp.float32)
    arrived = [swap(across[z].astype(jnp.bfloat16), 4 * z).astype(jnp.float32) for z in (3, 2, 1)]
    return across[0] + arrived[0] + arrived[1] + arrived[2]


def ring_shards(
    rhs_child,
    rhs_root,
    lower_kids,
    lower_couple,
    lower_root,
    upper_root,
    upper_couple,
    upper_kids,
    tile_pattern,
):
    root_rows = rhs_root.shape[0]
    position = lax.axis_index("col").astype(jnp.int32)
    place = position[None]
    root_tiles = root_rows // NB
    child_tiles = tile_pattern.shape[1]
    mine = lax.dynamic_slice(
        tile_pattern, (position * root_tiles, 0), (root_tiles, child_tiles)
    ).astype(jnp.bfloat16)
    lower_tiles = jnp.pad(jnp.repeat(mine, NB, axis=1), ((0, TILE_ROWS - root_tiles), (0, 0)))
    row_tiles = np.arange(root_rows)[:, None] // NB == np.arange(TILE_ROWS)[None, :]
    root_of = jnp.asarray(row_tiles.astype(np.float32), jnp.bfloat16)

    flat = lambda a: a.reshape(a.shape[0], -1)
    child_in = flat(rhs_child).astype(jnp.bfloat16)
    pieces, lower_tiles, root_base = lax.optimization_barrier(
        (gather_pieces(child_in), lower_tiles, flat(rhs_root))
    )
    child_lower, child_lower_b = fold(
        place, pieces, jnp.swapaxes(lower_kids, 1, 2), wide=True
    )
    (root_rhs_b,) = fold(
        place,
        gather_pieces(child_lower_b),
        jnp.swapaxes(lower_couple, 1, 2),
        mask=(root_of, lower_tiles),
        base=root_base,
    )
    (root_lower_b,) = fold(place, gather_pieces(root_rhs_b), lower_root)
    root_solution, root_solution_b = fold(
        place, gather_pieces(root_lower_b), upper_root, wide=True
    )
    keep, send = spread(place, root_solution_b, upper_couple, (root_of, lower_tiles))
    child_rhs_b = (child_lower - scatter_sum(keep, send)).astype(jnp.bfloat16)
    (child_solution,) = fold(
        place,
        gather_pieces(child_rhs_b),
        jnp.swapaxes(upper_kids, 1, 2),
        wide=True,
        narrow=False,
    )
    return (child_solution.reshape(rhs_child.shape), root_solution.reshape(rhs_root.shape))


def fits(devices, rhs_child, rhs_root, tile_pattern):
    root_rows = rhs_root.shape[0] // devices
    return (
        devices == GROUP
        and rhs_child.shape[0] % (devices * 8) == 0
        and rhs_root.shape[0] % (devices * NB) == 0
        and rhs_child.shape[0] % LANES == 0
        and rhs_root.shape[0] % LANES == 0
        and root_rows // NB <= TILE_ROWS
    )


def solution(mesh):
    in_specs = (
        P("col", None, None),
        P("col", None, None),
        P("pts", None, "col"),
        P("pts", None, "col"),
        P("pts", "col", None),
        P("pts", "col", None),
        P("pts", "col", None),
        P("pts", None, "col"),
        P(),
    )
    out_specs = (P(("pts", "col"), None, None), P(("pts", "col"), None, None))

    def whole(*args):
        body = ring_shards if fits(mesh.shape["col"], args[0], args[1], args[-1]) else general_shards
        return jax.shard_map(body, mesh=mesh, in_specs=in_specs, out_specs=out_specs, check_vma=False)(*args)

    return whole
```

```python
import functools

import jax
import jax.numpy as jnp
from jax import lax
from jax.experimental import pallas as pl
from jax.experimental.pallas import tpu as pltpu
from jax.sharding import PartitionSpec as P

NB = 16
GROUP = 16
LANES = 128
AHEAD = 3
VMEM = 44 * 1024 * 1024


def combine(product):
    return jnp.stack(
        [
            product[..., 0, 0, :] - product[..., 1, 1, :],
            product[..., 0, 1, :] + product[..., 1, 0, :],
        ],
        axis=-2,
    )


def column_fold(matrix, piece):
    return combine(jnp.einsum("aji,jbp->iabp", matrix, piece, preferred_element_type=jnp.float32))


def root_fold(matrix, piece):
    return combine(jnp.einsum("aic,cbp->iabp", matrix, piece, preferred_element_type=jnp.float32))


def general_shards(
    rhs_child,
    rhs_root,
    lower_kids,
    lower_couple,
    lower_root,
    upper_root,
    upper_couple,
    upper_kids,
    tile_pattern,
):
    root_rows = rhs_root.shape[0]
    position = lax.axis_index("col")
    pattern_f = tile_pattern.astype(jnp.float32)
    root_tiles = (position * root_rows + jnp.arange(root_rows, dtype=jnp.int32)) // NB
    root_onehot = (
        root_tiles[:, None] == jnp.arange(pattern_f.shape[0], dtype=jnp.int32)[None, :]
    ).astype(jnp.float32)
    couple_mask = jnp.repeat(jnp.dot(root_onehot, pattern_f), NB, axis=1)
    child_in = rhs_child.astype(jnp.bfloat16)
    child_lower = column_fold(lower_kids, lax.all_gather(child_in, "col", axis=0, tiled=True))
    child_lower_b = child_lower.astype(jnp.bfloat16)
    masked = lower_couple * jnp.transpose(couple_mask).astype(jnp.bfloat16)[None]
    coupling = column_fold(masked, lax.all_gather(child_lower_b, "col", axis=0, tiled=True))
    root_rhs_b = (rhs_root - coupling).astype(jnp.bfloat16)
    root_lower = root_fold(lower_root, lax.all_gather(root_rhs_b, "col", axis=0, tiled=True))
    root_lower_b = root_lower.astype(jnp.bfloat16)
    root_solution = root_fold(upper_root, lax.all_gather(root_lower_b, "col", axis=0, tiled=True))
    root_solution_b = root_solution.astype(jnp.bfloat16)
    masked = upper_couple * couple_mask.astype(jnp.bfloat16)[None]
    update = lax.psum_scatter(
        combine(
            jnp.einsum("aij,ibp->jabp", masked, root_solution_b, preferred_element_type=jnp.float32)
        ),
        "col",
        scatter_dimension=0,
        tiled=True,
    )
    child_rhs_b = (child_lower - update).astype(jnp.bfloat16)
    child_solution = column_fold(upper_kids, lax.all_gather(child_rhs_b, "col", axis=0, tiled=True))
    return (child_solution, root_solution)


def swap(x, bits):
    return lax.ppermute(x, "col", [(i, i ^ bits) for i in range(GROUP)])


def window_of(unit, rows):
    start = unit * rows
    into = lax.rem(start, LANES)
    return pl.multiple_of(start - into, LANES), pl.multiple_of(into, 16)


def span_of(rows):
    return -(-(rows + LANES - 16) // LANES) * LANES


def fold_kernel(flips, split, masked, first, residual, wide, narrow, *refs):
    refs = list(refs)
    place_ref = refs.pop(0)
    pieces = [refs.pop(0) for _ in range(len(flips) * split)]
    w_hbm = refs.pop(0)
    tiles_ref = refs.pop(0) if masked else None
    acc_in_ref = None if first else refs.pop(0)
    base_ref = refs.pop(0) if residual else None
    last = wide or narrow
    acc_out_ref = None if last else refs.pop(0)
    wide_ref = refs.pop(0) if wide else None
    narrow_ref = refs.pop(0) if narrow else None
    x_ref, w_ref, acc_ref, piece_sems, w_sems = refs[:5]
    stage_ref = refs[5] if split > 1 else None

    place = place_ref[0]
    rows = split * pieces[0].shape[0]
    span = x_ref.shape[1]
    here = place if split == 1 else place >> 1
    edge = LANES - 16

    def piece_copy(index):
        if split > 1:
            target = stage_ref.at[index]
        else:
            _, into = window_of(here ^ flips[index], rows)
            target = x_ref.at[index, pl.ds(into, rows), :]
        return pltpu.make_async_copy(pieces[index], target, piece_sems.at[index])

    def w_copy(index):
        start, _ = window_of(here ^ flips[index], rows)
        return pltpu.make_async_copy(
            w_hbm.at[:, :, pl.ds(start, span)], w_ref.at[index], w_sems.at[index]
        )

    def ready(index):
        if split == 1:
            piece_copy(index).wait()
            return
        piece_copy(2 * index).wait()
        piece_copy(2 * index + 1).wait()
        low = (place & 1) == 0
        mine = stage_ref[2 * index].astype(jnp.float32)
        other = stage_ref[2 * index + 1].astype(jnp.float32)
        pair = jnp.concatenate([jnp.where(low, mine, other), jnp.where(low, other, mine)], axis=0)
        _, into = window_of(here ^ flips[index], rows)
        x_ref[index, pl.ds(into, rows), :] = pair.astype(jnp.bfloat16)

    for index in range(min(AHEAD, len(flips))):
        w_copy(index).start()
    blank = jnp.zeros((edge, x_ref.shape[2]), jnp.bfloat16)
    for index in range(len(flips)):
        x_ref[index, :edge, :] = blank
        x_ref[index, span - edge :, :] = blank
    for index in range(len(pieces)):
        piece_copy(index).start()
    if first:
        acc_ref[...] = jnp.zeros_like(acc_ref)
    else:
        acc_ref[...] = acc_in_ref[...]
    for index in range(len(flips)):
        ready(index)
        w_copy(index).wait()
        if index + AHEAD < len(flips):
            w_copy(index + AHEAD).start()
        x = x_ref[index]
        if masked:
            start, _ = window_of(here ^ flips[index], rows)
            mask = mask_of(tiles_ref, start, span)
        for part in range(2):
            w = w_ref[index, part]
            if masked:
                w = w * mask
            acc_ref[part] += jnp.dot(w, x, preferred_element_type=jnp.float32)
    if not last:
        acc_out_ref[...] = acc_ref[...]
        return
    half = acc_ref.shape[2] // 2
    real = acc_ref[0, :, :half] - acc_ref[1, :, half:]
    imag = acc_ref[0, :, half:] + acc_ref[1, :, :half]
    if residual:
        real = base_ref[:, :half] - real
        imag = base_ref[:, half:] - imag
    for out in (wide_ref, narrow_ref):
        if out is not None:
            out[:, :half] = real.astype(out.dtype)
            out[:, half:] = imag.astype(out.dtype)


def fold_part(
    place, pieces, flips, split, matrix, tiles=None, acc=None, base=None, wide=False, narrow=False
):
    _, height, _ = matrix.shape
    rows, width = pieces[0].shape
    span = span_of(split * rows)
    units = len(flips)
    anywhere = pl.BlockSpec(memory_space=pl.ANY)
    vmem = pl.BlockSpec(memory_space=pltpu.VMEM)
    operands = [place, *pieces, matrix]
    specs = [pl.BlockSpec(memory_space=pltpu.SMEM)] + [anywhere] * (len(pieces) + 1)
    for extra in (tiles, acc, base):
        if extra is not None:
            operands.append(extra)
            specs.append(vmem)
    shapes = []
    if wide:
        shapes.append(jax.ShapeDtypeStruct((height, width), jnp.float32))
    if narrow:
        shapes.append(jax.ShapeDtypeStruct((height, width), jnp.bfloat16))
    if not shapes:
        shapes.append(jax.ShapeDtypeStruct((2, height, width), jnp.float32))
    scratch = [
        pltpu.VMEM((units, span, width), jnp.bfloat16),
        pltpu.VMEM((units, 2, height, span), jnp.bfloat16),
        pltpu.VMEM((2, height, width), jnp.float32),
        pltpu.SemaphoreType.DMA((len(pieces),)),
        pltpu.SemaphoreType.DMA((units,)),
    ]
    if split > 1:
        scratch.append(pltpu.VMEM((len(pieces), rows, width), jnp.bfloat16))
    return pl.pallas_call(
        functools.partial(
            fold_kernel, flips, split, tiles is not None, acc is None, base is not None, wide, narrow
        ),
        out_shape=shapes,
        in_specs=specs,
        out_specs=[vmem] * len(shapes),
        scratch_shapes=scratch,
        compiler_params=pltpu.CompilerParams(vmem_limit_bytes=VMEM),
        cost_estimate=pl.CostEstimate(
            flops=4 * units * span * height * width,
            bytes_accessed=4 * units * span * height,
            transcendentals=0,
        ),
    )(*operands)


EARLY = (0, 2, 4, 6, 8, 12)
LATE = (10, 14)


def gathered_fold(place, x, matrix, split, beside=None, tiles=None, **last):
    def part(chips, **rest):
        if split == 1:
            flips = tuple(m | core for m in chips for core in range(2))
        else:
            flips = tuple(m >> 1 for m in chips)
        given = [pieces[m | core] for m in chips for core in range(2)]
        return fold_part(place, given, flips, split, matrix, tiles=tiles, **rest)

    pieces = {0: x}
    for bits in (12, 8, 4):
        pieces[bits] = swap(x, bits)
    pieces[2] = swap(x, 2)
    extra = None
    if beside is not None:
        pieces[4], extra = lax.optimization_barrier((pieces[4], beside()))
    for bits in (4, 8, 12):
        pieces[bits | 2] = swap(pieces[bits], 2)
    for bits in (0, 2, 4, 8, 6, 12):
        pieces[bits | 1] = swap(pieces[bits], 1)
    (acc,) = part(EARLY)
    pieces[10], pieces[14], acc = lax.optimization_barrier((pieces[10], pieces[14], acc))
    for bits in (10, 14):
        pieces[bits | 1] = swap(pieces[bits], 1)
    return part(LATE, acc=acc, **last), extra


def widen_kernel(rows_ref, out_ref):
    tiles = rows_ref.shape[1]
    span = out_ref.shape[1]
    column = pl.program_id(0) * span + lax.broadcasted_iota(jnp.int32, (tiles, span), 1)
    tile = lax.broadcasted_iota(jnp.int32, (tiles, span), 0)
    chosen = jnp.where(column >> (NB.bit_length() - 1) == tile, 1.0, 0.0).astype(jnp.bfloat16)
    out_ref[...] = jnp.dot(rows_ref[...], chosen, preferred_element_type=jnp.float32)


def widen(pattern, length):
    span = 6 * LANES
    return pl.pallas_call(
        widen_kernel,
        grid=(pl.cdiv(length, span),),
        in_specs=[pl.BlockSpec(pattern.shape, lambda i: (0, 0))],
        out_specs=pl.BlockSpec((pattern.shape[0], span), lambda i: (0, i)),
        out_shape=jax.ShapeDtypeStruct((pattern.shape[0], length), jnp.float32),
        cost_estimate=pl.CostEstimate(
            flops=2 * pattern.size * length, bytes_accessed=4 * pattern.shape[0] * length, transcendentals=0
        ),
    )(pattern)


def mask_of(tiles_ref, start, span):
    tiles = tiles_ref[:, pl.ds(start, span)]
    count = tiles.shape[0]
    return jnp.broadcast_to(tiles[:, None, :], (count, NB, span)).reshape(count * NB, span).astype(jnp.bfloat16)


def spread_kernel(
    flips, place_ref, x_ref, w_hbm, tiles_ref, keep_ref, send_ref, w_ref, total_ref, w_sems
):
    place = place_ref[0]
    _, rows, width = keep_ref.shape
    half = width // 2
    span = w_ref.shape[3]

    def w_copy(index):
        start, _ = window_of((place >> 1) ^ flips[index], 2 * rows)
        return pltpu.make_async_copy(
            w_hbm.at[:, :, pl.ds(start, span)], w_ref.at[index], w_sems.at[index]
        )

    for index in range(min(AHEAD, len(flips))):
        w_copy(index).start()
    x = x_ref[...]
    low = (place & 1) == 0
    for index in range(len(flips)):
        w_copy(index).wait()
        if index + AHEAD < len(flips):
            w_copy(index + AHEAD).start()
        start, into = window_of((place >> 1) ^ flips[index], 2 * rows)
        mask = mask_of(tiles_ref, start, span)
        first, second = (
            lax.dot_general(
                w_ref[index, part] * mask,
                x,
                (((0,), (0,)), ((), ())),
                preferred_element_type=jnp.float32,
            )
            for part in range(2)
        )
        total_ref[index, :, :half] = first[:, :half] - second[:, half:]
        total_ref[index, :, half:] = first[:, half:] + second[:, :half]
        one = total_ref[index, pl.ds(into, rows), :]
        two = total_ref[index, pl.ds(pl.multiple_of(into + rows, 8), rows), :]
        keep_ref[index] = jnp.where(low, one, two)
        send_ref[index] = jnp.where(low, two, one).astype(send_ref.dtype)


def spread(place, x, matrix, tiles, flips):
    _, depth, length = matrix.shape
    rows = length // GROUP
    width = x.shape[1]
    span = span_of(2 * rows)
    units = len(flips)
    vmem = pl.BlockSpec(memory_space=pltpu.VMEM)
    block = (units, rows, width)
    return pl.pallas_call(
        functools.partial(spread_kernel, flips),
        out_shape=[
            jax.ShapeDtypeStruct(block, jnp.float32),
            jax.ShapeDtypeStruct(block, jnp.bfloat16),
        ],
        in_specs=[
            pl.BlockSpec(memory_space=pltpu.SMEM),
            vmem,
            pl.BlockSpec(memory_space=pl.ANY),
            vmem,
        ],
        out_specs=[vmem, vmem],
        scratch_shapes=[
            pltpu.VMEM((units, 2, depth, span), jnp.bfloat16),
            pltpu.VMEM((units, span, width), jnp.float32),
            pltpu.SemaphoreType.DMA((units,)),
        ],
        compiler_params=pltpu.CompilerParams(vmem_limit_bytes=VMEM),
        cost_estimate=pl.CostEstimate(
            flops=4 * units * span * depth * width,
            bytes_accessed=4 * units * span * depth,
            transcendentals=0,
        ),
    )(place, x, matrix, tiles)


def scatter_sum(place, x, matrix, tiles):
    across = {}
    for z in (3, 1):
        keep, send = spread(place, x, matrix, tiles, (2 * z, 2 * z + 1, 2 * z - 2, 2 * z - 1))
        for half in range(2):
            got = swap(send[2 * half : 2 * half + 2], 1).astype(jnp.float32)
            mine = keep[2 * half] + got[0]
            other = keep[2 * half + 1] + got[1]
            arrived = swap(other.astype(jnp.bfloat16), 2).astype(jnp.float32)
            across[z - half] = mine + arrived
    arrived = [swap(across[z].astype(jnp.bfloat16), 4 * z).astype(jnp.float32) for z in (3, 2, 1)]
    return across[0] + arrived[0] + arrived[1] + arrived[2]


def ring_shards(
    rhs_child,
    rhs_root,
    lower_kids,
    lower_couple,
    lower_root,
    upper_root,
    upper_couple,
    upper_kids,
    tile_pattern,
):
    root_rows = rhs_root.shape[0]
    position = lax.axis_index("col").astype(jnp.int32)
    place = position[None]
    root_tiles = root_rows // NB
    mine = lax.dynamic_slice(
        tile_pattern, (position * root_tiles, 0), (root_tiles, tile_pattern.shape[1])
    ).astype(jnp.bfloat16)

    flat = lambda a: a.reshape(a.shape[0], -1)
    (child_lower, child_lower_b), (tiles, root_base) = gathered_fold(
        place,
        flat(rhs_child).astype(jnp.bfloat16),
        jnp.swapaxes(lower_kids, 1, 2),
        2,
        beside=lambda: (widen(mine, lower_couple.shape[1]), flat(rhs_root)),
        wide=True,
        narrow=True,
    )
    (root_rhs_b,), _ = gathered_fold(
        place,
        child_lower_b,
        jnp.swapaxes(lower_couple, 1, 2),
        2,
        tiles=tiles,
        base=root_base,
        narrow=True,
    )
    (root_lower_b,), _ = gathered_fold(place, root_rhs_b, lower_root, 1, narrow=True)
    (root_solution, root_solution_b), _ = gathered_fold(
        place, root_lower_b, upper_root, 1, wide=True, narrow=True
    )
    update = scatter_sum(place, root_solution_b, upper_couple, tiles)
    (child_solution,), root_out = gathered_fold(
        place,
        (child_lower - update).astype(jnp.bfloat16),
        jnp.swapaxes(upper_kids, 1, 2),
        2,
        beside=lambda: root_solution.reshape(rhs_root.shape),
        wide=True,
    )
    return (child_solution.reshape(rhs_child.shape), root_out)


def fits(devices, child, root):
    pair, own = 2 * child // devices, root // devices
    within = all(
        rows % NB == 0
        and (index * rows) // LANES * LANES + span_of(rows) <= total
        for rows, total in ((pair, child), (own, root))
        for index in range(total // max(rows, 1))
    )
    return devices == GROUP and child % LANES == 0 and root % LANES == 0 and pair % NB == 0 and within


def solution(mesh):
    in_specs = (
        P("col", None, None),
        P("col", None, None),
        P("pts", None, "col"),
        P("pts", None, "col"),
        P("pts", "col", None),
        P("pts", "col", None),
        P("pts", "col", None),
        P("pts", None, "col"),
        P(),
    )
    out_specs = (P(("pts", "col"), None, None), P(("pts", "col"), None, None))

    def whole(*args):
        body = ring_shards if fits(mesh.shape["col"], args[0].shape[0], args[1].shape[0]) else general_shards
        return jax.shard_map(body, mesh=mesh, in_specs=in_specs, out_specs=out_specs, check_vma=False)(*args)

    return whole
```

```python
import functools

import jax
import jax.numpy as jnp
from jax import lax
from jax.experimental import pallas as pl
from jax.experimental.pallas import tpu as pltpu
from jax.sharding import PartitionSpec as P

NB = 16
GROUP = 16
LANES = 128
AHEAD = 3
VMEM = 44 * 1024 * 1024
MOST = 20 * 1024 * 1024


def combine(product):
    return jnp.stack(
        [
            product[..., 0, 0, :] - product[..., 1, 1, :],
            product[..., 0, 1, :] + product[..., 1, 0, :],
        ],
        axis=-2,
    )


def column_fold(matrix, piece):
    return combine(jnp.einsum("aji,jbp->iabp", matrix, piece, preferred_element_type=jnp.float32))


def root_fold(matrix, piece):
    return combine(jnp.einsum("aic,cbp->iabp", matrix, piece, preferred_element_type=jnp.float32))


def general_shards(
    rhs_child,
    rhs_root,
    lower_kids,
    lower_couple,
    lower_root,
    upper_root,
    upper_couple,
    upper_kids,
    tile_pattern,
):
    root_rows = rhs_root.shape[0]
    position = lax.axis_index("col")
    pattern_f = tile_pattern.astype(jnp.float32)
    root_tiles = (position * root_rows + jnp.arange(root_rows, dtype=jnp.int32)) // NB
    root_onehot = (
        root_tiles[:, None] == jnp.arange(pattern_f.shape[0], dtype=jnp.int32)[None, :]
    ).astype(jnp.float32)
    couple_mask = jnp.repeat(jnp.dot(root_onehot, pattern_f), NB, axis=1)
    child_in = rhs_child.astype(jnp.bfloat16)
    child_lower = column_fold(lower_kids, lax.all_gather(child_in, "col", axis=0, tiled=True))
    child_lower_b = child_lower.astype(jnp.bfloat16)
    masked = lower_couple * jnp.transpose(couple_mask).astype(jnp.bfloat16)[None]
    coupling = column_fold(masked, lax.all_gather(child_lower_b, "col", axis=0, tiled=True))
    root_rhs_b = (rhs_root - coupling).astype(jnp.bfloat16)
    root_lower = root_fold(lower_root, lax.all_gather(root_rhs_b, "col", axis=0, tiled=True))
    root_lower_b = root_lower.astype(jnp.bfloat16)
    root_solution = root_fold(upper_root, lax.all_gather(root_lower_b, "col", axis=0, tiled=True))
    root_solution_b = root_solution.astype(jnp.bfloat16)
    masked = upper_couple * couple_mask.astype(jnp.bfloat16)[None]
    update = lax.psum_scatter(
        combine(
            jnp.einsum("aij,ibp->jabp", masked, root_solution_b, preferred_element_type=jnp.float32)
        ),
        "col",
        scatter_dimension=0,
        tiled=True,
    )
    child_rhs_b = (child_lower - update).astype(jnp.bfloat16)
    child_solution = column_fold(upper_kids, lax.all_gather(child_rhs_b, "col", axis=0, tiled=True))
    return (child_solution, root_solution)


def swap(x, bits):
    return lax.ppermute(x, "col", [(i, i ^ bits) for i in range(GROUP)])


def window_of(unit, rows):
    start = unit * rows
    into = lax.rem(start, LANES)
    return pl.multiple_of(start - into, LANES), pl.multiple_of(into, 16)


def span_of(rows):
    return -(-(rows + LANES - 16) // LANES) * LANES


def fold_kernel(flips, split, masked, first, residual, wide, narrow, *refs):
    refs = list(refs)
    place_ref = refs.pop(0)
    pieces = [refs.pop(0) for _ in range(len(flips) * split)]
    w_hbm = refs.pop(0)
    tiles_ref = refs.pop(0) if masked else None
    acc_in_ref = None if first else refs.pop(0)
    base_ref = refs.pop(0) if residual else None
    last = wide or narrow
    acc_out_ref = None if last else refs.pop(0)
    wide_ref = refs.pop(0) if wide else None
    narrow_ref = refs.pop(0) if narrow else None
    x_ref, w_ref, acc_ref, piece_sems, w_sems = refs[:5]
    stage_ref = refs[5] if split > 1 else None

    place = place_ref[0]
    rows = split * pieces[0].shape[0]
    span = x_ref.shape[1]
    here = place if split == 1 else place >> 1
    edge = LANES - 16

    def piece_copy(index):
        if split > 1:
            target = stage_ref.at[index]
        else:
            _, into = window_of(here ^ flips[index], rows)
            target = x_ref.at[index, pl.ds(into, rows), :]
        return pltpu.make_async_copy(pieces[index], target, piece_sems.at[index])

    def w_copy(index):
        start, _ = window_of(here ^ flips[index], rows)
        return pltpu.make_async_copy(
            w_hbm.at[:, :, pl.ds(start, span)], w_ref.at[index], w_sems.at[index]
        )

    def ready(index):
        if split == 1:
            piece_copy(index).wait()
            return
        piece_copy(2 * index).wait()
        piece_copy(2 * index + 1).wait()
        low = (place & 1) == 0
        mine = stage_ref[2 * index].astype(jnp.float32)
        other = stage_ref[2 * index + 1].astype(jnp.float32)
        pair = jnp.concatenate([jnp.where(low, mine, other), jnp.where(low, other, mine)], axis=0)
        _, into = window_of(here ^ flips[index], rows)
        x_ref[index, pl.ds(into, rows), :] = pair.astype(jnp.bfloat16)

    for index in range(min(AHEAD, len(flips))):
        w_copy(index).start()
    blank = jnp.zeros((edge, x_ref.shape[2]), jnp.bfloat16)
    for index in range(len(flips)):
        x_ref[index, :edge, :] = blank
        x_ref[index, span - edge :, :] = blank
    for index in range(len(pieces)):
        piece_copy(index).start()
    if first:
        acc_ref[...] = jnp.zeros_like(acc_ref)
    else:
        acc_ref[...] = acc_in_ref[...]
    for index in range(len(flips)):
        ready(index)
        w_copy(index).wait()
        if index + AHEAD < len(flips):
            w_copy(index + AHEAD).start()
        x = x_ref[index]
        if masked:
            start, _ = window_of(here ^ flips[index], rows)
            mask = mask_of(tiles_ref, start, span)
        for part in range(2):
            w = w_ref[index, part]
            if masked:
                w = w * mask
            acc_ref[part] += jnp.dot(w, x, preferred_element_type=jnp.float32)
    if not last:
        acc_out_ref[...] = acc_ref[...]
        return
    half = acc_ref.shape[2] // 2
    real = acc_ref[0, :, :half] - acc_ref[1, :, half:]
    imag = acc_ref[0, :, half:] + acc_ref[1, :, :half]
    if residual:
        real = base_ref[:, :half] - real
        imag = base_ref[:, half:] - imag
    for out in (wide_ref, narrow_ref):
        if out is not None and len(out.shape) == 3:
            out[:, 0, :] = real
            out[:, 1, :] = imag
        elif out is not None:
            out[:, :half] = real.astype(out.dtype)
            out[:, half:] = imag.astype(out.dtype)


def fold_part(
    place, pieces, flips, split, matrix, tiles=None, acc=None, base=None, wide=False, narrow=False
):
    _, height, _ = matrix.shape
    rows, width = pieces[0].shape
    span = span_of(split * rows)
    units = len(flips)
    anywhere = pl.BlockSpec(memory_space=pl.ANY)
    vmem = pl.BlockSpec(memory_space=pltpu.VMEM)
    operands = [place, *pieces, matrix]
    specs = [pl.BlockSpec(memory_space=pltpu.SMEM)] + [anywhere] * (len(pieces) + 1)
    for extra in (tiles, acc, base):
        if extra is not None:
            operands.append(extra)
            specs.append(vmem)
    shapes = []
    if wide:
        shape = (height, width) if wide == "flat" else (height, 2, width // 2)
        shapes.append(jax.ShapeDtypeStruct(shape, jnp.float32))
    if narrow:
        shapes.append(jax.ShapeDtypeStruct((height, width), jnp.bfloat16))
    if not shapes:
        shapes.append(jax.ShapeDtypeStruct((2, height, width), jnp.float32))
    scratch = [
        pltpu.VMEM((units, span, width), jnp.bfloat16),
        pltpu.VMEM((units, 2, height, span), jnp.bfloat16),
        pltpu.VMEM((2, height, width), jnp.float32),
        pltpu.SemaphoreType.DMA((len(pieces),)),
        pltpu.SemaphoreType.DMA((units,)),
    ]
    if split > 1:
        scratch.append(pltpu.VMEM((len(pieces), rows, width), jnp.bfloat16))
    return pl.pallas_call(
        functools.partial(
            fold_kernel, flips, split, tiles is not None, acc is None, base is not None, wide, narrow
        ),
        out_shape=shapes,
        in_specs=specs,
        out_specs=[vmem] * len(shapes),
        scratch_shapes=scratch,
        compiler_params=pltpu.CompilerParams(
            vmem_limit_bytes=MOST if split > 1 and tiles is None else VMEM
        ),
        cost_estimate=pl.CostEstimate(
            flops=4 * units * span * height * width,
            bytes_accessed=4 * units * span * height,
            transcendentals=0,
        ),
    )(*operands)


ORDER = ((0, 2, 4, 8, 6, 12), (10, 14))


def gathered_fold(place, x, matrix, split, beside=None, tiles=None, base=None, **last):
    def part(chips, acc, **rest):
        if split == 1:
            flips = tuple(m | core for m in chips for core in range(2))
        else:
            flips = tuple(m >> 1 for m in chips)
        given = [pieces[m | core] for m in chips for core in range(2)]
        return fold_part(place, given, flips, split, matrix, tiles=tiles, acc=acc, **rest)

    pieces = {0: x}
    for bits in (4, 8, 2):
        pieces[bits] = swap(x, bits)
    extra = None
    if beside is not None:
        pieces[4], extra = lax.optimization_barrier((pieces[4], beside()))
    pieces[6] = swap(pieces[4], 2)
    pieces[12] = swap(pieces[8], 4)
    following, pieces[6] = lax.optimization_barrier((pieces[8], pieces[6]))
    pieces[10] = swap(following, 2)
    for bits in (0, 2, 4, 8, 6):
        pieces[bits | 1] = swap(pieces[bits], 1)
    pieces[14] = swap(pieces[12], 2)
    pieces[13] = swap(pieces[12], 1)
    acc = None
    for chips, following in zip(ORDER, ORDER[1:]):
        (acc,) = part(chips, acc)
        *held, acc = lax.optimization_barrier((*(pieces[m] for m in following), acc))
        for m, piece in zip(following, held):
            pieces[m] = piece
            pieces[m | 1] = swap(piece, 1)
    return part(ORDER[-1], acc, base=base, **last), extra


def widen_kernel(rows_ref, out_ref):
    tiles = rows_ref.shape[1]
    span = out_ref.shape[1]
    column = pl.program_id(0) * span + lax.broadcasted_iota(jnp.int32, (tiles, span), 1)
    tile = lax.broadcasted_iota(jnp.int32, (tiles, span), 0)
    chosen = jnp.where(column >> (NB.bit_length() - 1) == tile, 1.0, 0.0).astype(jnp.bfloat16)
    out_ref[...] = jnp.dot(rows_ref[...], chosen, preferred_element_type=jnp.float32)


def widen(pattern, length):
    span = 6 * LANES
    return pl.pallas_call(
        widen_kernel,
        grid=(pl.cdiv(length, span),),
        in_specs=[pl.BlockSpec(pattern.shape, lambda i: (0, 0))],
        out_specs=pl.BlockSpec((pattern.shape[0], span), lambda i: (0, i)),
        out_shape=jax.ShapeDtypeStruct((pattern.shape[0], length), jnp.float32),
        cost_estimate=pl.CostEstimate(
            flops=2 * pattern.size * length, bytes_accessed=4 * pattern.shape[0] * length, transcendentals=0
        ),
    )(pattern)


def mask_of(tiles_ref, start, span):
    tiles = tiles_ref[:, pl.ds(start, span)]
    count = tiles.shape[0]
    return jnp.broadcast_to(tiles[:, None, :], (count, NB, span)).reshape(count * NB, span).astype(jnp.bfloat16)


def spread_kernel(
    flips, place_ref, x_ref, w_hbm, tiles_ref, keep_ref, send_ref, w_ref, total_ref, w_sems
):
    place = place_ref[0]
    _, rows, width = keep_ref.shape
    half = width // 2
    span = w_ref.shape[3]

    def w_copy(index):
        start, _ = window_of((place >> 1) ^ flips[index], 2 * rows)
        return pltpu.make_async_copy(
            w_hbm.at[:, :, pl.ds(start, span)], w_ref.at[index], w_sems.at[index]
        )

    for index in range(min(AHEAD, len(flips))):
        w_copy(index).start()
    x = x_ref[...]
    low = (place & 1) == 0
    for index in range(len(flips)):
        w_copy(index).wait()
        if index + AHEAD < len(flips):
            w_copy(index + AHEAD).start()
        start, into = window_of((place >> 1) ^ flips[index], 2 * rows)
        mask = mask_of(tiles_ref, start, span)
        first, second = (
            lax.dot_general(
                w_ref[index, part] * mask,
                x,
                (((0,), (0,)), ((), ())),
                preferred_element_type=jnp.float32,
            )
            for part in range(2)
        )
        total_ref[index, :, :half] = first[:, :half] - second[:, half:]
        total_ref[index, :, half:] = first[:, half:] + second[:, :half]
        one = total_ref[index, pl.ds(into, rows), :]
        two = total_ref[index, pl.ds(pl.multiple_of(into + rows, 8), rows), :]
        keep_ref[index] = jnp.where(low, one, two)
        send_ref[index] = jnp.where(low, two, one).astype(send_ref.dtype)


def spread(place, x, matrix, tiles, flips):
    _, depth, length = matrix.shape
    rows = length // GROUP
    width = x.shape[1]
    span = span_of(2 * rows)
    units = len(flips)
    vmem = pl.BlockSpec(memory_space=pltpu.VMEM)
    block = (units, rows, width)
    return pl.pallas_call(
        functools.partial(spread_kernel, flips),
        out_shape=[
            jax.ShapeDtypeStruct(block, jnp.float32),
            jax.ShapeDtypeStruct(block, jnp.bfloat16),
        ],
        in_specs=[
            pl.BlockSpec(memory_space=pltpu.SMEM),
            vmem,
            pl.BlockSpec(memory_space=pl.ANY),
            vmem,
        ],
        out_specs=[vmem, vmem],
        scratch_shapes=[
            pltpu.VMEM((units, 2, depth, span), jnp.bfloat16),
            pltpu.VMEM((units, span, width), jnp.float32),
            pltpu.SemaphoreType.DMA((units,)),
        ],
        compiler_params=pltpu.CompilerParams(vmem_limit_bytes=VMEM),
        cost_estimate=pl.CostEstimate(
            flops=4 * units * span * depth * width,
            bytes_accessed=4 * units * span * depth,
            transcendentals=0,
        ),
    )(place, x, matrix, tiles)


def scatter_sum(place, x, matrix, tiles):
    across, mine, other = {}, {}, {}
    for z in (3, 1):
        keep, send = spread(place, x, matrix, tiles, (2 * z, 2 * z + 1, 2 * z - 2, 2 * z - 1))
        for half in range(2):
            got = swap(send[2 * half : 2 * half + 2], 1).astype(jnp.float32)
            mine[z - half] = keep[2 * half] + got[0]
            other[z - half] = (keep[2 * half + 1] + got[1]).astype(jnp.bfloat16)
        if z == 3:
            x, other[3], other[2] = lax.optimization_barrier((x, other[3], other[2]))
        for half in range(2):
            across[z - half] = mine[z - half] + swap(other[z - half], 2).astype(jnp.float32)
    arrived = [swap(across[z].astype(jnp.bfloat16), 4 * z).astype(jnp.float32) for z in (3, 2, 1)]
    return across[0] + arrived[0] + arrived[1] + arrived[2]


def ring_shards(
    rhs_child,
    rhs_root,
    lower_kids,
    lower_couple,
    lower_root,
    upper_root,
    upper_couple,
    upper_kids,
    tile_pattern,
):
    root_rows = rhs_root.shape[0]
    position = lax.axis_index("col").astype(jnp.int32)
    place = position[None]
    root_tiles = root_rows // NB
    mine = lax.dynamic_slice(
        tile_pattern, (position * root_tiles, 0), (root_tiles, tile_pattern.shape[1])
    ).astype(jnp.bfloat16)

    flat = lambda a: a.reshape(a.shape[0], -1)
    (child_lower, child_lower_b), (tiles, root_base) = gathered_fold(
        place,
        flat(rhs_child).astype(jnp.bfloat16),
        jnp.swapaxes(lower_kids, 1, 2),
        2,
        beside=lambda: (widen(mine, lower_couple.shape[1]), flat(rhs_root)),
        wide="flat",
        narrow=True,
    )
    (root_rhs_b,), _ = gathered_fold(
        place,
        child_lower_b,
        jnp.swapaxes(lower_couple, 1, 2),
        2,
        tiles=tiles,
        base=root_base,
        narrow=True,
    )
    (root_lower_b,), _ = gathered_fold(place, root_rhs_b, lower_root, 1, narrow=True)
    (root_solution, root_solution_b), _ = gathered_fold(
        place, root_lower_b, upper_root, 1, wide="parts", narrow=True
    )
    update = scatter_sum(place, root_solution_b, upper_couple, tiles)
    (child_solution,), _ = gathered_fold(
        place,
        (child_lower - update).astype(jnp.bfloat16),
        jnp.swapaxes(upper_kids, 1, 2),
        2,
        wide="parts",
    )
    return (child_solution, root_solution)


def fits(devices, child, root):
    pair, own = 2 * child // devices, root // devices
    within = all(
        rows % NB == 0
        and (index * rows) // LANES * LANES + span_of(rows) <= total
        for rows, total in ((pair, child), (own, root))
        for index in range(total // max(rows, 1))
    )
    return devices == GROUP and child % LANES == 0 and root % LANES == 0 and pair % NB == 0 and within


def solution(mesh):
    in_specs = (
        P("col", None, None),
        P("col", None, None),
        P("pts", None, "col"),
        P("pts", None, "col"),
        P("pts", "col", None),
        P("pts", "col", None),
        P("pts", "col", None),
        P("pts", None, "col"),
        P(),
    )
    out_specs = (P(("pts", "col"), None, None), P(("pts", "col"), None, None))

    def whole(*args):
        body = ring_shards if fits(mesh.shape["col"], args[0].shape[0], args[1].shape[0]) else general_shards
        return jax.shard_map(body, mesh=mesh, in_specs=in_specs, out_specs=out_specs, check_vma=False)(*args)

    return whole
```

```python
import functools

import jax
import jax.numpy as jnp
from jax import lax
from jax.experimental import pallas as pl
from jax.experimental.pallas import tpu as pltpu
from jax.sharding import PartitionSpec as P

NB = 16
GROUP = 16
LANES = 128
AHEAD = 3
VMEM = 40 * 1024 * 1024
MOST = 20 * 1024 * 1024


def combine(product):
    return jnp.stack(
        [
            product[..., 0, 0, :] - product[..., 1, 1, :],
            product[..., 0, 1, :] + product[..., 1, 0, :],
        ],
        axis=-2,
    )


def column_fold(matrix, piece):
    return combine(jnp.einsum("aji,jbp->iabp", matrix, piece, preferred_element_type=jnp.float32))


def root_fold(matrix, piece):
    return combine(jnp.einsum("aic,cbp->iabp", matrix, piece, preferred_element_type=jnp.float32))


def general_shards(
    rhs_child,
    rhs_root,
    lower_kids,
    lower_couple,
    lower_root,
    upper_root,
    upper_couple,
    upper_kids,
    tile_pattern,
):
    root_rows = rhs_root.shape[0]
    position = lax.axis_index("col")
    pattern_f = tile_pattern.astype(jnp.float32)
    root_tiles = (position * root_rows + jnp.arange(root_rows, dtype=jnp.int32)) // NB
    root_onehot = (
        root_tiles[:, None] == jnp.arange(pattern_f.shape[0], dtype=jnp.int32)[None, :]
    ).astype(jnp.float32)
    couple_mask = jnp.repeat(jnp.dot(root_onehot, pattern_f), NB, axis=1)
    child_in = rhs_child.astype(jnp.bfloat16)
    child_lower = column_fold(lower_kids, lax.all_gather(child_in, "col", axis=0, tiled=True))
    child_lower_b = child_lower.astype(jnp.bfloat16)
    masked = lower_couple * jnp.transpose(couple_mask).astype(jnp.bfloat16)[None]
    coupling = column_fold(masked, lax.all_gather(child_lower_b, "col", axis=0, tiled=True))
    root_rhs_b = (rhs_root - coupling).astype(jnp.bfloat16)
    root_lower = root_fold(lower_root, lax.all_gather(root_rhs_b, "col", axis=0, tiled=True))
    root_lower_b = root_lower.astype(jnp.bfloat16)
    root_solution = root_fold(upper_root, lax.all_gather(root_lower_b, "col", axis=0, tiled=True))
    root_solution_b = root_solution.astype(jnp.bfloat16)
    masked = upper_couple * couple_mask.astype(jnp.bfloat16)[None]
    update = lax.psum_scatter(
        combine(
            jnp.einsum("aij,ibp->jabp", masked, root_solution_b, preferred_element_type=jnp.float32)
        ),
        "col",
        scatter_dimension=0,
        tiled=True,
    )
    child_rhs_b = (child_lower - update).astype(jnp.bfloat16)
    child_solution = column_fold(upper_kids, lax.all_gather(child_rhs_b, "col", axis=0, tiled=True))
    return (child_solution, root_solution)


def swap(x, bits):
    return lax.ppermute(x, "col", [(i, i ^ bits) for i in range(GROUP)])


def window_of(unit, rows):
    start = unit * rows
    into = lax.rem(start, LANES)
    return pl.multiple_of(start - into, LANES), pl.multiple_of(into, 16)


def span_of(rows):
    return -(-(rows + LANES - 16) // LANES) * LANES


def fold_kernel(flips, after, stocked, split, masked, first, residual, wide, narrow, *refs):
    refs = list(refs)
    place_ref = refs.pop(0)
    pieces = [refs.pop(0) for _ in range(len(flips) * split)]
    w_hbm = refs.pop(0)
    stock_in_ref = refs.pop(0) if stocked else None
    tiles_ref = refs.pop(0) if masked else None
    acc_in_ref = None if first else refs.pop(0)
    base_ref = refs.pop(0) if residual else None
    last = wide or narrow
    acc_out_ref = None if last else refs.pop(0)
    stock_out_ref = refs.pop(0) if after else None
    wide_ref = refs.pop(0) if wide else None
    narrow_ref = refs.pop(0) if narrow else None
    x_ref, acc_ref, piece_sems, w_sems = refs[:4]
    refs = refs[4:]
    w_ref = stock_in_ref if stocked else refs.pop(0)
    stage_ref = refs.pop(0) if split > 1 else None
    stock_sems = refs.pop(0) if after else None

    place = place_ref[0]
    rows = split * pieces[0].shape[0]
    span = x_ref.shape[1]
    here = place if split == 1 else place >> 1
    edge = LANES - 16

    def piece_copy(index):
        if split > 1:
            target = stage_ref.at[index]
        else:
            _, into = window_of(here ^ flips[index], rows)
            target = x_ref.at[index, pl.ds(into, rows), :]
        return pltpu.make_async_copy(pieces[index], target, piece_sems.at[index])

    def w_copy(index):
        start, _ = window_of(here ^ flips[index], rows)
        return pltpu.make_async_copy(
            w_hbm.at[:, :, pl.ds(start, span)], w_ref.at[index], w_sems.at[index]
        )

    def stock_copy(index):
        start, _ = window_of(here ^ after[index], rows)
        return pltpu.make_async_copy(
            w_hbm.at[:, :, pl.ds(start, span)], stock_out_ref.at[index], stock_sems.at[index]
        )

    def ready(index):
        if split == 1:
            piece_copy(index).wait()
            return
        piece_copy(2 * index).wait()
        piece_copy(2 * index + 1).wait()
        low = (place & 1) == 0
        mine = stage_ref[2 * index].astype(jnp.float32)
        other = stage_ref[2 * index + 1].astype(jnp.float32)
        pair = jnp.concatenate([jnp.where(low, mine, other), jnp.where(low, other, mine)], axis=0)
        _, into = window_of(here ^ flips[index], rows)
        x_ref[index, pl.ds(into, rows), :] = pair.astype(jnp.bfloat16)

    for index in range(0 if stocked else min(AHEAD, len(flips))):
        w_copy(index).start()
    blank = jnp.zeros((edge, x_ref.shape[2]), jnp.bfloat16)
    for index in range(len(flips)):
        x_ref[index, :edge, :] = blank
        x_ref[index, span - edge :, :] = blank
    for index in range(len(pieces)):
        piece_copy(index).start()
    if first:
        acc_ref[...] = jnp.zeros_like(acc_ref)
    else:
        acc_ref[...] = acc_in_ref[...]
    for index in range(len(flips)):
        ready(index)
        if not stocked:
            w_copy(index).wait()
        if index + AHEAD < len(flips) and not stocked:
            w_copy(index + AHEAD).start()
        elif index + AHEAD - len(flips) in range(len(after)):
            stock_copy(index + AHEAD - len(flips)).start()
        x = x_ref[index]
        if masked:
            start, _ = window_of(here ^ flips[index], rows)
            mask = mask_of(tiles_ref, start, span)
        for part in range(2):
            w = w_ref[index, part]
            if masked:
                w = w * mask
            acc_ref[part] += jnp.dot(w, x, preferred_element_type=jnp.float32)
    if not last:
        acc_out_ref[...] = acc_ref[...]
        for index in range(AHEAD, len(after)):
            stock_copy(index).start()
        for index in range(len(after)):
            stock_copy(index).wait()
        return
    half = acc_ref.shape[2] // 2
    real = acc_ref[0, :, :half] - acc_ref[1, :, half:]
    imag = acc_ref[0, :, half:] + acc_ref[1, :, :half]
    if residual:
        real = base_ref[:, :half] - real
        imag = base_ref[:, half:] - imag
    for out in (wide_ref, narrow_ref):
        if out is not None and len(out.shape) == 3:
            out[:, 0, :] = real
            out[:, 1, :] = imag
        elif out is not None:
            out[:, :half] = real.astype(out.dtype)
            out[:, half:] = imag.astype(out.dtype)


def fold_part(
    place, pieces, flips, split, matrix, after=(), stock=None, tiles=None, acc=None, base=None, wide=False, narrow=False
):
    _, height, _ = matrix.shape
    rows, width = pieces[0].shape
    span = span_of(split * rows)
    units = len(flips)
    anywhere = pl.BlockSpec(memory_space=pl.ANY)
    vmem = pl.BlockSpec(memory_space=pltpu.VMEM)
    operands = [place, *pieces, matrix]
    specs = [pl.BlockSpec(memory_space=pltpu.SMEM)] + [anywhere] * (len(pieces) + 1)
    for extra in (stock, tiles, acc, base):
        if extra is not None:
            operands.append(extra)
            specs.append(vmem)
    shapes = []
    if wide:
        shape = (height, width) if wide == "flat" else (height, 2, width // 2)
        shapes.append(jax.ShapeDtypeStruct(shape, jnp.float32))
    if narrow:
        shapes.append(jax.ShapeDtypeStruct((height, width), jnp.bfloat16))
    if not shapes:
        shapes.append(jax.ShapeDtypeStruct((2, height, width), jnp.float32))
    results = [vmem] * len(shapes)
    if after:
        shapes.append(jax.ShapeDtypeStruct((len(after), 2, height, span), jnp.bfloat16))
        results.append(anywhere)
    scratch = [
        pltpu.VMEM((units, span, width), jnp.bfloat16),
        pltpu.VMEM((2, height, width), jnp.float32),
        pltpu.SemaphoreType.DMA((len(pieces),)),
        pltpu.SemaphoreType.DMA((units,)),
    ]
    if stock is None:
        scratch.append(pltpu.VMEM((units, 2, height, span), jnp.bfloat16))
    if split > 1:
        scratch.append(pltpu.VMEM((len(pieces), rows, width), jnp.bfloat16))
    if after:
        scratch.append(pltpu.SemaphoreType.DMA((len(after),)))
    return pl.pallas_call(
        functools.partial(
            fold_kernel,
            flips,
            after,
            stock is not None,
            split,
            tiles is not None,
            acc is None,
            base is not None,
            wide,
            narrow,
        ),
        out_shape=shapes,
        in_specs=specs,
        out_specs=results,
        scratch_shapes=scratch,
        compiler_params=pltpu.CompilerParams(
            vmem_limit_bytes=MOST if split > 1 and tiles is None else VMEM
        ),
        cost_estimate=pl.CostEstimate(
            flops=4 * units * span * height * width,
            bytes_accessed=4 * units * span * height,
            transcendentals=0,
        ),
    )(*operands)


ORDER = ((0, 2, 4, 8, 6, 12), (10, 14))


def gathered_fold(place, x, matrix, split, beside=None, tiles=None, base=None, **last):
    def flips_of(chips):
        if split == 1:
            return tuple(m | core for m in chips for core in range(2))
        return tuple(m >> 1 for m in chips)

    def part(chips, acc, **rest):
        given = [pieces[m | core] for m in chips for core in range(2)]
        return fold_part(place, given, flips_of(chips), split, matrix, tiles=tiles, acc=acc, **rest)

    pieces = {0: x}
    for bits in (4, 8, 2):
        pieces[bits] = swap(x, bits)
    extra = None
    if beside is not None:
        pieces[4], extra = lax.optimization_barrier((pieces[4], beside()))
    pieces[6] = swap(pieces[4], 2)
    pieces[12] = swap(pieces[8], 4)
    following, pieces[6] = lax.optimization_barrier((pieces[8], pieces[6]))
    pieces[10] = swap(following, 2)
    for bits in (0, 2, 4, 8, 6):
        pieces[bits | 1] = swap(pieces[bits], 1)
    pieces[14] = swap(pieces[12], 2)
    pieces[13] = swap(pieces[12], 1)
    acc = stock = None
    for chips, following in zip(ORDER, ORDER[1:]):
        if split == 1:
            acc, stock = part(chips, acc, after=flips_of(following))
        else:
            (acc,) = part(chips, acc)
        *held, acc = lax.optimization_barrier((*(pieces[m] for m in following), acc))
        for m, piece in zip(following, held):
            pieces[m] = piece
            pieces[m | 1] = swap(piece, 1)
    return part(ORDER[-1], acc, stock=stock, base=base, **last), extra


def widen_kernel(rows_ref, out_ref):
    tiles = rows_ref.shape[1]
    span = out_ref.shape[1]
    column = pl.program_id(0) * span + lax.broadcasted_iota(jnp.int32, (tiles, span), 1)
    tile = lax.broadcasted_iota(jnp.int32, (tiles, span), 0)
    chosen = jnp.where(column >> (NB.bit_length() - 1) == tile, 1.0, 0.0).astype(jnp.bfloat16)
    out_ref[...] = jnp.dot(rows_ref[...], chosen, preferred_element_type=jnp.float32)


def widen(pattern, length):
    span = 6 * LANES
    return pl.pallas_call(
        widen_kernel,
        grid=(pl.cdiv(length, span),),
        in_specs=[pl.BlockSpec(pattern.shape, lambda i: (0, 0))],
        out_specs=pl.BlockSpec((pattern.shape[0], span), lambda i: (0, i)),
        out_shape=jax.ShapeDtypeStruct((pattern.shape[0], length), jnp.float32),
        cost_estimate=pl.CostEstimate(
            flops=2 * pattern.size * length, bytes_accessed=4 * pattern.shape[0] * length, transcendentals=0
        ),
    )(pattern)


def mask_of(tiles_ref, start, span):
    tiles = tiles_ref[:, pl.ds(start, span)]
    count = tiles.shape[0]
    return jnp.broadcast_to(tiles[:, None, :], (count, NB, span)).reshape(count * NB, span).astype(jnp.bfloat16)


def spread_kernel(
    flips, place_ref, x_ref, w_hbm, tiles_ref, keep_ref, send_ref, w_ref, total_ref, w_sems
):
    place = place_ref[0]
    _, rows, width = keep_ref.shape
    half = width // 2
    span = w_ref.shape[3]

    def w_copy(index):
        start, _ = window_of((place >> 1) ^ flips[index], 2 * rows)
        return pltpu.make_async_copy(
            w_hbm.at[:, :, pl.ds(start, span)], w_ref.at[index], w_sems.at[index]
        )

    for index in range(min(AHEAD, len(flips))):
        w_copy(index).start()
    x = x_ref[...]
    low = (place & 1) == 0
    for index in range(len(flips)):
        w_copy(index).wait()
        if index + AHEAD < len(flips):
            w_copy(index + AHEAD).start()
        start, into = window_of((place >> 1) ^ flips[index], 2 * rows)
        mask = mask_of(tiles_ref, start, span)
        first, second = (
            lax.dot_general(
                w_ref[index, part] * mask,
                x,
                (((0,), (0,)), ((), ())),
                preferred_element_type=jnp.float32,
            )
            for part in range(2)
        )
        total_ref[index, :, :half] = first[:, :half] - second[:, half:]
        total_ref[index, :, half:] = first[:, half:] + second[:, :half]
        one = total_ref[index, pl.ds(into, rows), :]
        two = total_ref[index, pl.ds(pl.multiple_of(into + rows, 8), rows), :]
        keep_ref[index] = jnp.where(low, one, two)
        send_ref[index] = jnp.where(low, two, one).astype(send_ref.dtype)


def spread(place, x, matrix, tiles, flips):
    _, depth, length = matrix.shape
    rows = length // GROUP
    width = x.shape[1]
    span = span_of(2 * rows)
    units = len(flips)
    vmem = pl.BlockSpec(memory_space=pltpu.VMEM)
    block = (units, rows, width)
    return pl.pallas_call(
        functools.partial(spread_kernel, flips),
        out_shape=[
            jax.ShapeDtypeStruct(block, jnp.float32),
            jax.ShapeDtypeStruct(block, jnp.bfloat16),
        ],
        in_specs=[
            pl.BlockSpec(memory_space=pltpu.SMEM),
            vmem,
            pl.BlockSpec(memory_space=pl.ANY),
            vmem,
        ],
        out_specs=[vmem, vmem],
        scratch_shapes=[
            pltpu.VMEM((units, 2, depth, span), jnp.bfloat16),
            pltpu.VMEM((units, span, width), jnp.float32),
            pltpu.SemaphoreType.DMA((units,)),
        ],
        compiler_params=pltpu.CompilerParams(vmem_limit_bytes=VMEM),
        cost_estimate=pl.CostEstimate(
            flops=4 * units * span * depth * width,
            bytes_accessed=4 * units * span * depth,
            transcendentals=0,
        ),
    )(place, x, matrix, tiles)


def scatter_sum(place, x, matrix, tiles):
    across, mine, other = {}, {}, {}
    for z in (3, 1):
        keep, send = spread(place, x, matrix, tiles, (2 * z, 2 * z + 1, 2 * z - 2, 2 * z - 1))
        for half in range(2):
            got = swap(send[2 * half : 2 * half + 2], 1).astype(jnp.float32)
            mine[z - half] = keep[2 * half] + got[0]
            other[z - half] = (keep[2 * half + 1] + got[1]).astype(jnp.bfloat16)
        if z == 3:
            x, other[3], other[2] = lax.optimization_barrier((x, other[3], other[2]))
        for half in range(2):
            across[z - half] = mine[z - half] + swap(other[z - half], 2).astype(jnp.float32)
    arrived = [swap(across[z].astype(jnp.bfloat16), 4 * z).astype(jnp.float32) for z in (3, 2, 1)]
    return across[0] + arrived[0] + arrived[1] + arrived[2]


def ring_shards(
    rhs_child,
    rhs_root,
    lower_kids,
    lower_couple,
    lower_root,
    upper_root,
    upper_couple,
    upper_kids,
    tile_pattern,
):
    root_rows = rhs_root.shape[0]
    position = lax.axis_index("col").astype(jnp.int32)
    place = position[None]
    root_tiles = root_rows // NB
    mine = lax.dynamic_slice(
        tile_pattern, (position * root_tiles, 0), (root_tiles, tile_pattern.shape[1])
    ).astype(jnp.bfloat16)

    flat = lambda a: a.reshape(a.shape[0], -1)
    (child_lower, child_lower_b), (tiles, root_base) = gathered_fold(
        place,
        flat(rhs_child).astype(jnp.bfloat16),
        jnp.swapaxes(lower_kids, 1, 2),
        2,
        beside=lambda: (widen(mine, lower_couple.shape[1]), flat(rhs_root)),
        wide="flat",
        narrow=True,
    )
    (root_rhs_b,), _ = gathered_fold(
        place,
        child_lower_b,
        jnp.swapaxes(lower_couple, 1, 2),
        2,
        tiles=tiles,
        base=root_base,
        narrow=True,
    )
    (root_lower_b,), _ = gathered_fold(place, root_rhs_b, lower_root, 1, narrow=True)
    (root_solution, root_solution_b), _ = gathered_fold(
        place, root_lower_b, upper_root, 1, wide="flat", narrow=True
    )
    update = scatter_sum(place, root_solution_b, upper_couple, tiles)
    (child_solution,), root_solution = gathered_fold(
        place,
        (child_lower - update).astype(jnp.bfloat16),
        jnp.swapaxes(upper_kids, 1, 2),
        2,
        beside=lambda: root_solution.reshape(rhs_root.shape),
        wide="parts",
    )
    return (child_solution, root_solution)


def fits(devices, child, root):
    pair, own = 2 * child // devices, root // devices
    within = all(
        rows % NB == 0
        and (index * rows) // LANES * LANES + span_of(rows) <= total
        for rows, total in ((pair, child), (own, root))
        for index in range(total // max(rows, 1))
    )
    return devices == GROUP and child % LANES == 0 and root % LANES == 0 and pair % NB == 0 and within


def solution(mesh):
    in_specs = (
        P("col", None, None),
        P("col", None, None),
        P("pts", None, "col"),
        P("pts", None, "col"),
        P("pts", "col", None),
        P("pts", "col", None),
        P("pts", "col", None),
        P("pts", None, "col"),
        P(),
    )
    out_specs = (P(("pts", "col"), None, None), P(("pts", "col"), None, None))

    def whole(*args):
        body = ring_shards if fits(mesh.shape["col"], args[0].shape[0], args[1].shape[0]) else general_shards
        return jax.shard_map(body, mesh=mesh, in_specs=in_specs, out_specs=out_specs, check_vma=False)(*args)

    return whole
```

```python
import functools

import jax
import jax.numpy as jnp
from jax import lax
from jax.experimental import pallas as pl
from jax.experimental.pallas import tpu as pltpu
from jax.sharding import PartitionSpec as P

NB = 16
GROUP = 16
LANES = 128
AHEAD = 2
VMEM = 40 * 1024 * 1024
MOST = 20 * 1024 * 1024


def combine(product):
    return jnp.stack(
        [
            product[..., 0, 0, :] - product[..., 1, 1, :],
            product[..., 0, 1, :] + product[..., 1, 0, :],
        ],
        axis=-2,
    )


def column_fold(matrix, piece):
    return combine(jnp.einsum("aji,jbp->iabp", matrix, piece, preferred_element_type=jnp.float32))


def root_fold(matrix, piece):
    return combine(jnp.einsum("aic,cbp->iabp", matrix, piece, preferred_element_type=jnp.float32))


def general_shards(
    rhs_child,
    rhs_root,
    lower_kids,
    lower_couple,
    lower_root,
    upper_root,
    upper_couple,
    upper_kids,
    tile_pattern,
):
    root_rows = rhs_root.shape[0]
    position = lax.axis_index("col")
    pattern_f = tile_pattern.astype(jnp.float32)
    root_tiles = (position * root_rows + jnp.arange(root_rows, dtype=jnp.int32)) // NB
    root_onehot = (
        root_tiles[:, None] == jnp.arange(pattern_f.shape[0], dtype=jnp.int32)[None, :]
    ).astype(jnp.float32)
    couple_mask = jnp.repeat(jnp.dot(root_onehot, pattern_f), NB, axis=1)
    child_in = rhs_child.astype(jnp.bfloat16)
    child_lower = column_fold(lower_kids, lax.all_gather(child_in, "col", axis=0, tiled=True))
    child_lower_b = child_lower.astype(jnp.bfloat16)
    masked = lower_couple * jnp.transpose(couple_mask).astype(jnp.bfloat16)[None]
    coupling = column_fold(masked, lax.all_gather(child_lower_b, "col", axis=0, tiled=True))
    root_rhs_b = (rhs_root - coupling).astype(jnp.bfloat16)
    root_lower = root_fold(lower_root, lax.all_gather(root_rhs_b, "col", axis=0, tiled=True))
    root_lower_b = root_lower.astype(jnp.bfloat16)
    root_solution = root_fold(upper_root, lax.all_gather(root_lower_b, "col", axis=0, tiled=True))
    root_solution_b = root_solution.astype(jnp.bfloat16)
    masked = upper_couple * couple_mask.astype(jnp.bfloat16)[None]
    update = lax.psum_scatter(
        combine(
            jnp.einsum("aij,ibp->jabp", masked, root_solution_b, preferred_element_type=jnp.float32)
        ),
        "col",
        scatter_dimension=0,
        tiled=True,
    )
    child_rhs_b = (child_lower - update).astype(jnp.bfloat16)
    child_solution = column_fold(upper_kids, lax.all_gather(child_rhs_b, "col", axis=0, tiled=True))
    return (child_solution, root_solution)


def swap(x, bits):
    return lax.ppermute(x, "col", [(i, i ^ bits) for i in range(GROUP)])


def window_of(unit, rows):
    start = unit * rows
    into = lax.rem(start, LANES)
    return pl.multiple_of(start - into, LANES), pl.multiple_of(into, 16)


def span_of(rows):
    return -(-(rows + LANES - 16) // LANES) * LANES


def fold_kernel(flips, after, stocked, split, masked, first, residual, wide, narrow, *refs):
    refs = list(refs)
    place_ref = refs.pop(0)
    pieces = [refs.pop(0) for _ in range(len(flips) * split)]
    w_hbm = refs.pop(0)
    stock_in_ref = refs.pop(0) if stocked else None
    tiles_ref = refs.pop(0) if masked else None
    acc_in_ref = None if first else refs.pop(0)
    base_ref = refs.pop(0) if residual else None
    last = wide or narrow
    acc_out_ref = None if last else refs.pop(0)
    stock_out_ref = refs.pop(0) if after else None
    wide_ref = refs.pop(0) if wide else None
    narrow_ref = refs.pop(0) if narrow else None
    x_ref, acc_ref, piece_sems, w_sems = refs[:4]
    refs = refs[4:]
    w_ref = stock_in_ref if stocked else refs.pop(0)
    stage_ref = refs.pop(0) if split > 1 else None
    stock_sems = refs.pop(0) if after else None

    place = place_ref[0]
    rows = split * pieces[0].shape[0]
    span = x_ref.shape[1]
    here = place if split == 1 else place >> 1
    edge = LANES - 16

    def piece_copy(index):
        if split > 1:
            target = stage_ref.at[index]
        else:
            _, into = window_of(here ^ flips[index], rows)
            target = x_ref.at[index, pl.ds(into, rows), :]
        return pltpu.make_async_copy(pieces[index], target, piece_sems.at[index])

    def w_copy(index):
        start, _ = window_of(here ^ flips[index], rows)
        return pltpu.make_async_copy(
            w_hbm.at[:, :, pl.ds(start, span)], w_ref.at[index], w_sems.at[index]
        )

    def stock_copy(index):
        start, _ = window_of(here ^ after[index], rows)
        return pltpu.make_async_copy(
            w_hbm.at[:, :, pl.ds(start, span)], stock_out_ref.at[index], stock_sems.at[index]
        )

    def ready(index):
        if split == 1:
            piece_copy(index).wait()
            return
        piece_copy(2 * index).wait()
        piece_copy(2 * index + 1).wait()
        low = (place & 1) == 0
        mine = stage_ref[2 * index].astype(jnp.float32)
        other = stage_ref[2 * index + 1].astype(jnp.float32)
        pair = jnp.concatenate([jnp.where(low, mine, other), jnp.where(low, other, mine)], axis=0)
        _, into = window_of(here ^ flips[index], rows)
        x_ref[index, pl.ds(into, rows), :] = pair.astype(jnp.bfloat16)

    for index in range(0 if stocked else min(AHEAD, len(flips))):
        w_copy(index).start()
    blank = jnp.zeros((edge, x_ref.shape[2]), jnp.bfloat16)
    for index in range(len(flips)):
        x_ref[index, :edge, :] = blank
        x_ref[index, span - edge :, :] = blank
    for index in range(len(pieces)):
        piece_copy(index).start()
    if first:
        acc_ref[...] = jnp.zeros_like(acc_ref)
    else:
        acc_ref[...] = acc_in_ref[...]
    for index in range(len(flips)):
        ready(index)
        if not stocked:
            w_copy(index).wait()
        if index + AHEAD < len(flips) and not stocked:
            w_copy(index + AHEAD).start()
        elif index + AHEAD - len(flips) in range(len(after)):
            stock_copy(index + AHEAD - len(flips)).start()
        x = x_ref[index]
        if masked:
            start, _ = window_of(here ^ flips[index], rows)
            mask = mask_of(tiles_ref, start, span)
        for part in range(2):
            w = w_ref[index, part]
            if masked:
                w = w * mask
            acc_ref[part] += jnp.dot(w, x, preferred_element_type=jnp.float32)
    if not last:
        acc_out_ref[...] = acc_ref[...]
        for index in range(AHEAD, len(after)):
            stock_copy(index).start()
        for index in range(len(after)):
            stock_copy(index).wait()
        return
    half = acc_ref.shape[2] // 2
    real = acc_ref[0, :, :half] - acc_ref[1, :, half:]
    imag = acc_ref[0, :, half:] + acc_ref[1, :, :half]
    if residual:
        real = base_ref[:, :half] - real
        imag = base_ref[:, half:] - imag
    for out in (wide_ref, narrow_ref):
        if out is not None and len(out.shape) == 3:
            out[:, 0, :] = real
            out[:, 1, :] = imag
        elif out is not None:
            out[:, :half] = real.astype(out.dtype)
            out[:, half:] = imag.astype(out.dtype)


def fold_part(
    place, pieces, flips, split, matrix, after=(), stock=None, tiles=None, acc=None, base=None, wide=False, narrow=False
):
    _, height, _ = matrix.shape
    rows, width = pieces[0].shape
    span = span_of(split * rows)
    units = len(flips)
    anywhere = pl.BlockSpec(memory_space=pl.ANY)
    vmem = pl.BlockSpec(memory_space=pltpu.VMEM)
    operands = [place, *pieces, matrix]
    specs = [pl.BlockSpec(memory_space=pltpu.SMEM)] + [anywhere] * (len(pieces) + 1)
    for extra in (stock, tiles, acc, base):
        if extra is not None:
            operands.append(extra)
            specs.append(vmem)
    shapes = []
    if wide:
        shape = (height, width) if wide == "flat" else (height, 2, width // 2)
        shapes.append(jax.ShapeDtypeStruct(shape, jnp.float32))
    if narrow:
        shapes.append(jax.ShapeDtypeStruct((height, width), jnp.bfloat16))
    if not shapes:
        shapes.append(jax.ShapeDtypeStruct((2, height, width), jnp.float32))
    results = [vmem] * len(shapes)
    if after:
        shapes.append(jax.ShapeDtypeStruct((len(after), 2, height, span), jnp.bfloat16))
        results.append(anywhere)
    scratch = [
        pltpu.VMEM((units, span, width), jnp.bfloat16),
        pltpu.VMEM((2, height, width), jnp.float32),
        pltpu.SemaphoreType.DMA((len(pieces),)),
        pltpu.SemaphoreType.DMA((units,)),
    ]
    if stock is None:
        scratch.append(pltpu.VMEM((units, 2, height, span), jnp.bfloat16))
    if split > 1:
        scratch.append(pltpu.VMEM((len(pieces), rows, width), jnp.bfloat16))
    if after:
        scratch.append(pltpu.SemaphoreType.DMA((len(after),)))
    return pl.pallas_call(
        functools.partial(
            fold_kernel,
            flips,
            after,
            stock is not None,
            split,
            tiles is not None,
            acc is None,
            base is not None,
            wide,
            narrow,
        ),
        out_shape=shapes,
        in_specs=specs,
        out_specs=results,
        scratch_shapes=scratch,
        compiler_params=pltpu.CompilerParams(
            vmem_limit_bytes=MOST if split > 1 and tiles is None else VMEM
        ),
        cost_estimate=pl.CostEstimate(
            flops=4 * units * span * height * width,
            bytes_accessed=4 * units * span * height,
            transcendentals=0,
        ),
    )(*operands)


ORDER = ((0, 2, 4, 8, 6, 12), (10, 14))


def gathered_fold(place, x, matrix, split, beside=None, tiles=None, base=None, **last):
    def flips_of(chips):
        if split == 1:
            return tuple(m | core for m in chips for core in range(2))
        return tuple(m >> 1 for m in chips)

    def part(chips, acc, **rest):
        given = [pieces[m | core] for m in chips for core in range(2)]
        return fold_part(place, given, flips_of(chips), split, matrix, tiles=tiles, acc=acc, **rest)

    pieces = {0: x}
    for bits in (4, 8, 2):
        pieces[bits] = swap(x, bits)
    extra = None
    if beside is not None:
        pieces[4], extra = lax.optimization_barrier((pieces[4], beside()))
    pieces[6] = swap(pieces[4], 2)
    pieces[12] = swap(pieces[8], 4)
    following, pieces[6] = lax.optimization_barrier((pieces[8], pieces[6]))
    pieces[10] = swap(following, 2)
    for bits in (0, 2, 4, 8, 6):
        pieces[bits | 1] = swap(pieces[bits], 1)
    pieces[14] = swap(pieces[12], 2)
    pieces[13] = swap(pieces[12], 1)
    acc = stock = None
    for chips, following in zip(ORDER, ORDER[1:]):
        if split == 1:
            acc, stock = part(chips, acc, after=flips_of(following))
        else:
            (acc,) = part(chips, acc)
        *held, acc = lax.optimization_barrier((*(pieces[m] for m in following), acc))
        for m, piece in zip(following, held):
            pieces[m] = piece
            pieces[m | 1] = swap(piece, 1)
    return part(ORDER[-1], acc, stock=stock, base=base, **last), extra


def widen_kernel(rows_ref, out_ref):
    tiles = rows_ref.shape[1]
    span = out_ref.shape[1]
    column = pl.program_id(0) * span + lax.broadcasted_iota(jnp.int32, (tiles, span), 1)
    tile = lax.broadcasted_iota(jnp.int32, (tiles, span), 0)
    chosen = jnp.where(column >> (NB.bit_length() - 1) == tile, 1.0, 0.0).astype(jnp.bfloat16)
    out_ref[...] = jnp.dot(rows_ref[...], chosen, preferred_element_type=jnp.float32)


def widen(pattern, length):
    span = 6 * LANES
    return pl.pallas_call(
        widen_kernel,
        grid=(pl.cdiv(length, span),),
        in_specs=[pl.BlockSpec(pattern.shape, lambda i: (0, 0))],
        out_specs=pl.BlockSpec((pattern.shape[0], span), lambda i: (0, i)),
        out_shape=jax.ShapeDtypeStruct((pattern.shape[0], length), jnp.float32),
        cost_estimate=pl.CostEstimate(
            flops=2 * pattern.size * length, bytes_accessed=4 * pattern.shape[0] * length, transcendentals=0
        ),
    )(pattern)


def mask_of(tiles_ref, start, span):
    tiles = tiles_ref[:, pl.ds(start, span)]
    count = tiles.shape[0]
    return jnp.broadcast_to(tiles[:, None, :], (count, NB, span)).reshape(count * NB, span).astype(jnp.bfloat16)


def spread_kernel(
    flips, place_ref, x_ref, w_hbm, tiles_ref, keep_ref, send_ref, w_ref, total_ref, w_sems
):
    place = place_ref[0]
    _, rows, width = keep_ref.shape
    half = width // 2
    span = w_ref.shape[3]

    def w_copy(index):
        start, _ = window_of((place >> 1) ^ flips[index], 2 * rows)
        return pltpu.make_async_copy(
            w_hbm.at[:, :, pl.ds(start, span)], w_ref.at[index], w_sems.at[index]
        )

    for index in range(min(AHEAD, len(flips))):
        w_copy(index).start()
    x = x_ref[...]
    low = (place & 1) == 0
    for index in range(len(flips)):
        w_copy(index).wait()
        if index + AHEAD < len(flips):
            w_copy(index + AHEAD).start()
        start, into = window_of((place >> 1) ^ flips[index], 2 * rows)
        mask = mask_of(tiles_ref, start, span)
        first, second = (
            lax.dot_general(
                w_ref[index, part] * mask,
                x,
                (((0,), (0,)), ((), ())),
                preferred_element_type=jnp.float32,
            )
            for part in range(2)
        )
        total_ref[index, :, :half] = first[:, :half] - second[:, half:]
        total_ref[index, :, half:] = first[:, half:] + second[:, :half]
        one = total_ref[index, pl.ds(into, rows), :]
        two = total_ref[index, pl.ds(pl.multiple_of(into + rows, 8), rows), :]
        keep_ref[index] = jnp.where(low, one, two)
        send_ref[index] = jnp.where(low, two, one).astype(send_ref.dtype)


def spread(place, x, matrix, tiles, flips):
    _, depth, length = matrix.shape
    rows = length // GROUP
    width = x.shape[1]
    span = span_of(2 * rows)
    units = len(flips)
    vmem = pl.BlockSpec(memory_space=pltpu.VMEM)
    block = (units, rows, width)
    return pl.pallas_call(
        functools.partial(spread_kernel, flips),
        out_shape=[
            jax.ShapeDtypeStruct(block, jnp.float32),
            jax.ShapeDtypeStruct(block, jnp.bfloat16),
        ],
        in_specs=[
            pl.BlockSpec(memory_space=pltpu.SMEM),
            vmem,
            pl.BlockSpec(memory_space=pl.ANY),
            vmem,
        ],
        out_specs=[vmem, vmem],
        scratch_shapes=[
            pltpu.VMEM((units, 2, depth, span), jnp.bfloat16),
            pltpu.VMEM((units, span, width), jnp.float32),
            pltpu.SemaphoreType.DMA((units,)),
        ],
        compiler_params=pltpu.CompilerParams(vmem_limit_bytes=VMEM),
        cost_estimate=pl.CostEstimate(
            flops=4 * units * span * depth * width,
            bytes_accessed=4 * units * span * depth,
            transcendentals=0,
        ),
    )(place, x, matrix, tiles)


def scatter_sum(place, x, matrix, tiles):
    across, mine, other = {}, {}, {}
    for z in (3, 1):
        keep, send = spread(place, x, matrix, tiles, (2 * z, 2 * z + 1, 2 * z - 2, 2 * z - 1))
        for half in range(2):
            got = swap(send[2 * half : 2 * half + 2], 1).astype(jnp.float32)
            mine[z - half] = keep[2 * half] + got[0]
            other[z - half] = (keep[2 * half + 1] + got[1]).astype(jnp.bfloat16)
        if z == 3:
            x, other[3], other[2] = lax.optimization_barrier((x, other[3], other[2]))
        for half in range(2):
            across[z - half] = mine[z - half] + swap(other[z - half], 2).astype(jnp.float32)
    arrived = [swap(across[z].astype(jnp.bfloat16), 4 * z).astype(jnp.float32) for z in (3, 2, 1)]
    return across[0] + arrived[0] + arrived[1] + arrived[2]


def ring_shards(
    rhs_child,
    rhs_root,
    lower_kids,
    lower_couple,
    lower_root,
    upper_root,
    upper_couple,
    upper_kids,
    tile_pattern,
):
    root_rows = rhs_root.shape[0]
    position = lax.axis_index("col").astype(jnp.int32)
    place = position[None]
    root_tiles = root_rows // NB
    mine = lax.dynamic_slice(
        tile_pattern, (position * root_tiles, 0), (root_tiles, tile_pattern.shape[1])
    ).astype(jnp.bfloat16)

    flat = lambda a: a.reshape(a.shape[0], -1)
    (child_lower, child_lower_b), (tiles, root_base) = gathered_fold(
        place,
        flat(rhs_child).astype(jnp.bfloat16),
        jnp.swapaxes(lower_kids, 1, 2),
        2,
        beside=lambda: (widen(mine, lower_couple.shape[1]), flat(rhs_root)),
        wide="flat",
        narrow=True,
    )
    (root_rhs_b,), _ = gathered_fold(
        place,
        child_lower_b,
        jnp.swapaxes(lower_couple, 1, 2),
        2,
        tiles=tiles,
        base=root_base,
        narrow=True,
    )
    (root_lower_b,), _ = gathered_fold(place, root_rhs_b, lower_root, 1, narrow=True)
    (root_solution, root_solution_b), _ = gathered_fold(
        place, root_lower_b, upper_root, 1, wide="flat", narrow=True
    )
    update = scatter_sum(place, root_solution_b, upper_couple, tiles)
    (child_solution,), root_solution = gathered_fold(
        place,
        (child_lower - update).astype(jnp.bfloat16),
        jnp.swapaxes(upper_kids, 1, 2),
        2,
        beside=lambda: root_solution.reshape(rhs_root.shape),
        wide="parts",
    )
    return (child_solution, root_solution)


def fits(devices, child, root):
    pair, own = 2 * child // devices, root // devices
    within = all(
        rows % NB == 0
        and (index * rows) // LANES * LANES + span_of(rows) <= total
        for rows, total in ((pair, child), (own, root))
        for index in range(total // max(rows, 1))
    )
    return devices == GROUP and child % LANES == 0 and root % LANES == 0 and pair % NB == 0 and within


def solution(mesh):
    in_specs = (
        P("col", None, None),
        P("col", None, None),
        P("pts", None, "col"),
        P("pts", None, "col"),
        P("pts", "col", None),
        P("pts", "col", None),
        P("pts", "col", None),
        P("pts", None, "col"),
        P(),
    )
    out_specs = (P(("pts", "col"), None, None), P(("pts", "col"), None, None))

    def whole(*args):
        body = ring_shards if fits(mesh.shape["col"], args[0].shape[0], args[1].shape[0]) else general_shards
        return jax.shard_map(body, mesh=mesh, in_specs=in_specs, out_specs=out_specs, check_vma=False)(*args)

    return whole
```
